32 devices in a mesh: gx: 8 (over y, x, core), gy: 4 (over z).
Axes of the slice: x: 2, y: 2, z: 4, core: 2. Of those that a mesh axis runs over, the one named last changes fastest.
Arguments:
- state_field: bfloat16 [192, 64, 1024], P(None, 'gy', 'gx'), may hold values from -6 to 6
- cotangent: bfloat16 [192, 64, 1024], P(None, 'gy', 'gx'), may hold values from -6 to 6
- ocean_mask: int32 [64, 1024], P('gy', 'gx'), may hold values from 0 to 1, as said below
- kernel: float32 [192, 7, 7], replicated, may hold values from -0.875 to 0.875
- inward_weight: bfloat16 [192, 768], replicated, may hold values from -0.4375 to 0.4375
- inward_bias: float32 [768], replicated, may hold values from -3 to 3
- outward_weight: bfloat16 [768, 192], replicated, may hold values from -0.21875 to 0.21875
- layer_scale: float32 [192], replicated, may hold values from 0.1 to 1.9
Outputs:
- output_field: bfloat16 [192, 64, 1024], P(None, 'gy', 'gx')
- field_grad: bfloat16 [192, 64, 1024], P(None, 'gy', 'gx')
- kernel_grad: float32 [192, 7, 7], replicated
- inward_grad: float32 [192, 768], replicated
- outward_grad: float32 [768, 192], replicated
The draws below stay inside these ranges and needn't reach their ends.
Inputs may be any that keep to these rules, and one draw needn't show every extreme that they name: `ocean_mask`: land comes as whole blocks of 4 latitude rows by the 128 columns of one device, and as single cells.
All inputs are finite; a program needn't handle non-finite values.
Results may differ from the reference program's by a relative error of at most 0.0064.
Values may be sent and summed in bfloat16 or wider, within the bound.
A program may use at most 64 MiB of HBM per device.

```python
import math
import jax
import jax.numpy as jnp
from jax import lax

C = 192
FF = 768
HT = 16
WT = 128
NLAT = 64
NLON = 1024


def draw_ocean_mask(key, part):
    block_rows = NLAT // 4
    block_cols = NLON // WT
    coarse_key = jax.random.fold_in(key, 11)
    speck_key = jax.random.fold_in(key, 12)
    coarse = jax.random.randint(coarse_key, (block_rows, block_cols), 0, 16)
    column = jnp.arange(block_cols, dtype=jnp.int32)
    limits = 2 + column % 8
    land_block = coarse < limits[None, :]
    block_full = jnp.repeat(jnp.repeat(land_block, 4, axis=0), WT, axis=1)
    speck = jax.random.randint(speck_key, (NLAT, NLON), 0, 6) == 0
    return jnp.where(block_full | speck, 0, 1).astype(jnp.int32)


def shard_levels(own_key, dims, cuts, smallest, high):
    def one(dim, shards_of):
        heights = jax.random.uniform(jax.random.fold_in(jax.random.fold_in(own_key, 6), dim), (shards_of,), jnp.float32, smallest / len(cuts), high / len(cuts))
        return jnp.repeat(jnp.exp(heights), dims[dim] // shards_of).reshape((-1,) + (1,) * (len(dims) - dim - 1))

    level = one(*cuts[0])
    for cut in cuts[1:]:
        level = level * one(*cut)
    return level


def centred(rng, extent, spread, bound, shards=(), kind=jnp.bfloat16):
    entries = spread * jax.random.normal(rng, extent, jnp.float32)
    if shards:
        entries = entries * shard_levels(rng, extent, shards, -0.22, 0.18)
    return jnp.clip(entries, -bound, bound).astype(kind)


def setup_inputs(seed: int = 0) -> dict:
    keys = jax.random.split(jax.random.key(seed), 9)
    return {
        "state_field": centred(keys[0], (C, NLAT, NLON), 1.0, 6.0, ((1, 4), (2, 8))),
        "cotangent": centred(keys[1], (C, NLAT, NLON), 1.0, 6.0, ((1, 4), (2, 8))),
        "ocean_mask": draw_ocean_mask(jax.random.fold_in(keys[8], 71), 0),
        "kernel": centred(keys[3], (C, 7, 7), 49 ** -0.5, 0.875, (), jnp.float32),
        "inward_weight": centred(keys[4], (C, FF), C ** -0.5, 0.4375),
        "inward_bias": centred(keys[5], (FF,), 0.5, 3.0, (), jnp.float32),
        "outward_weight": centred(keys[6], (FF, C), FF ** -0.5, 0.21875),
        "layer_scale": jnp.clip(1.0 + 0.18 * jax.random.normal(keys[7], (C,), jnp.float32), 0.1, 1.9),
    }


def gelu_value(values):
    return 0.5 * values * (1.0 + jax.scipy.special.erf(values / math.sqrt(2.0)))

def gelu_slope(values):
    return 0.5 * (1.0 + jax.scipy.special.erf(values / math.sqrt(2.0))) + values * jnp.exp(-0.5 * values * values) / math.sqrt(2.0 * math.pi)

def extend(source):
    wrapped = jnp.concatenate([source[:, :, -3:], source, source[:, :, :3]], axis=2)
    southern = jnp.zeros((source.shape[0], 3, wrapped.shape[2]), source.dtype)
    northern = jnp.flip(wrapped[:, -3:, :], (1, 2))
    return jnp.concatenate([southern, wrapped, northern], axis=1)

def group_conv(padded, kernel, flipped):
    lat_cells = padded.shape[1] - 6
    lon_cells = padded.shape[2] - 6
    summed = jnp.zeros((padded.shape[0], lat_cells, lon_cells), jnp.float32)
    for row_tap in range(7):
        for col_tap in range(7):
            if flipped:
                weights = kernel[:, 6 - row_tap, 6 - col_tap]
            else:
                weights = kernel[:, row_tap, col_tap]
            window = padded[:, row_tap:row_tap + lat_cells, col_tap:col_tap + lon_cells].astype(jnp.float32)
            summed = summed + weights[:, None, None] * window
    return summed

def grouped_conv(padded, kernel, flipped):
    groups = C // 16
    pad_groups = padded.reshape((groups, 16) + padded.shape[1:])
    ker_groups = kernel.reshape(groups, 16, 7, 7)
    results = lax.map(lambda operands: group_conv(operands[0], operands[1], flipped), (pad_groups, ker_groups))
    return results.reshape((C,) + results.shape[2:])

def group_kernel(grad_half, padded):
    lat_cells = grad_half.shape[1]
    lon_cells = grad_half.shape[2]
    grad_float = grad_half.astype(jnp.float32)
    row_sums = []
    for row_tap in range(7):
        column_sums = []
        for col_tap in range(7):
            window = padded[:, row_tap:row_tap + lat_cells, col_tap:col_tap + lon_cells].astype(jnp.float32)
            column_sums.append(lax.optimization_barrier(jnp.sum(grad_float * window, axis=(1, 2))))
        row_sums.append(jnp.stack(column_sums, axis=1))
    return jnp.stack(row_sums, axis=1)

def mlp_block(conv_out, field_blk, cot_blk, mask_blk, inward_weight, inward_bias, outward_weight, layer_scale):
    average = lax.optimization_barrier(jnp.mean(conv_out, axis=0, keepdims=True))
    centered = conv_out - average
    variance = lax.optimization_barrier(jnp.mean(centered * centered, axis=0, keepdims=True))
    inverse = lax.rsqrt(variance + 1e-06)
    normed = centered * inverse
    normed_half = normed.astype(jnp.bfloat16)
    contract = (((0,), (0,)), ((), ()))
    pre_act = lax.dot_general(inward_weight, normed_half, contract, preferred_element_type=jnp.float32) + inward_bias[:, None]
    hidden = gelu_value(pre_act).astype(jnp.bfloat16)
    branch = lax.dot_general(outward_weight, hidden, contract, preferred_element_type=jnp.float32)
    output_blk = (mask_blk * (field_blk.astype(jnp.float32) + layer_scale[:, None] * branch)).astype(jnp.bfloat16)
    masked_grad = mask_blk * cot_blk.astype(jnp.float32)
    branch_grad = (layer_scale[:, None] * masked_grad).astype(jnp.bfloat16)
    rows_contract = (((1,), (1,)), ((), ()))
    outward_part = lax.dot_general(hidden, branch_grad, rows_contract, preferred_element_type=jnp.float32)
    hidden_grad = jnp.dot(outward_weight, branch_grad, preferred_element_type=jnp.float32)
    pre_grad = (hidden_grad * gelu_slope(pre_act)).astype(jnp.bfloat16)
    inward_part = lax.dot_general(normed_half, pre_grad, rows_contract, preferred_element_type=jnp.float32)
    normed_grad = jnp.dot(inward_weight, pre_grad, preferred_element_type=jnp.float32)
    mean_grad = lax.optimization_barrier(jnp.mean(normed_grad, axis=0, keepdims=True))
    mean_prod = lax.optimization_barrier(jnp.mean(normed_grad * normed, axis=0, keepdims=True))
    conv_grad = (inverse * (normed_grad - mean_grad - normed * mean_prod)).astype(jnp.bfloat16)
    return (output_blk, conv_grad, inward_part, outward_part)

def reference(state_field, cotangent, ocean_mask, kernel, inward_weight, inward_bias, outward_weight, layer_scale):
    padded = extend(state_field)
    conv_out = grouped_conv(padded, kernel, False)
    mask_float = ocean_mask.astype(jnp.float32)
    block_count = NLAT // 4
    block_cells = 4 * NLON

    def scan_step(state_tuple, block_index):
        acc_in, acc_out = state_tuple
        offset = (block_index * 4).astype(jnp.int32)
        conv_blk = lax.dynamic_slice_in_dim(conv_out, offset, 4, 1).reshape(C, block_cells)
        field_blk = lax.dynamic_slice_in_dim(state_field, offset, 4, 1).reshape(C, block_cells)
        cot_blk = lax.dynamic_slice_in_dim(cotangent, offset, 4, 1).reshape(C, block_cells)
        mask_blk = lax.dynamic_slice_in_dim(mask_float, offset, 4, 0).reshape(1, block_cells)
        output_blk, conv_grad, inward_part, outward_part = mlp_block(conv_blk, field_blk, cot_blk, mask_blk, inward_weight, inward_bias, outward_weight, layer_scale)
        return ((acc_in + inward_part, acc_out + outward_part), (output_blk.reshape(C, 4, NLON), conv_grad.reshape(C, 4, NLON)))
    start_state = (jnp.zeros((C, FF), jnp.float32), jnp.zeros((FF, C), jnp.float32))
    (acc_in, acc_out), (out_blocks, grad_blocks) = lax.scan(scan_step, start_state, jnp.arange(block_count, dtype=jnp.int32))
    output_field = jnp.moveaxis(out_blocks, 0, 1).reshape(C, NLAT, NLON)
    conv_grad = jnp.moveaxis(grad_blocks, 0, 1).reshape(C, NLAT, NLON)
    factor = 1.0 / math.sqrt(HT * WT)
    grad_padded = extend(conv_grad)
    masked_grad = mask_float[None, :, :] * cotangent.astype(jnp.float32)
    field_grad = (masked_grad + grouped_conv(grad_padded, kernel, True)).astype(jnp.bfloat16)
    groups = C // 16
    grad_groups = conv_grad.reshape((groups, 16) + conv_grad.shape[1:])
    pad_groups = padded.reshape((groups, 16) + padded.shape[1:])
    kernel_parts = lax.map(lambda operands: group_kernel(operands[0], operands[1]), (grad_groups, pad_groups))
    kernel_grad = kernel_parts.reshape(C, 7, 7) * factor
    return (output_field, field_grad, kernel_grad, acc_in * factor, acc_out * factor)
```

```python
import math

import jax
import jax.numpy as jnp
from jax import lax
from jax.experimental import pallas as pl
from jax.experimental.pallas import tpu as pltpu
from jax.sharding import PartitionSpec as P

ROWS = 4
GROUP = 16
LANES = 128
WIDE = 256
F32 = jnp.float32
BF16 = jnp.bfloat16


def extend(rows):
    height, channels, width = rows.shape
    nx = lax.axis_size("gx")
    ny = lax.axis_size("gy")
    top = rows[height - 3 :]
    bottom = rows[:3]
    south = lax.ppermute(top, "gy", [(i, i + 1) for i in range(ny - 1)])
    north = lax.ppermute(bottom, "gy", [(i + 1, i) for i in range(ny - 1)])
    last = ny - 1
    facing = lax.ppermute(
        top, ("gx", "gy"), [(i * ny + last, (nx - 1 - i) * ny + last) for i in range(nx)]
    )
    turn = jnp.flip(jnp.eye(width, dtype=BF16), 0)
    turned = jnp.dot(facing[::-1].reshape(3 * channels, width), turn, preferred_element_type=F32)
    north = north + turned.astype(BF16).reshape(3, channels, width)
    tall = jnp.concatenate([south, rows, north], axis=0)

    def pack(part):
        return jnp.transpose(part, (0, 2, 1)).reshape((height + 6) * 3, channels)

    def unpack(part):
        return jnp.transpose(part.reshape(height + 6, 3, channels), (0, 2, 1))

    left = lax.ppermute(
        pack(tall[:, :, width - 3 :]), "gx", [(i, (i + 1) % nx) for i in range(nx)]
    )
    right = lax.ppermute(pack(tall[:, :, :3]), "gx", [((i + 1) % nx, i) for i in range(nx)])
    spare = jnp.zeros((height + 6, channels, WIDE - width - 6), BF16)
    return jnp.concatenate([unpack(left), tall, unpack(right), spare], axis=2)


def spread_taps(kernel_ref, taps_ref, flipped):
    table = kernel_ref[...]
    for tap in range(49):
        source = 48 - tap if flipped else tap
        taps_ref[tap] = jnp.broadcast_to(table[:, source : source + 1], taps_ref.shape[1:])


def shift_rows(ext_ref, shifted_ref):
    def one_row(row, carry):
        wide = ext_ref[row].astype(F32)
        for tap in range(7):
            moved = wide if tap == 0 else pltpu.roll(wide, WIDE - tap, 1)
            shifted_ref[tap, row] = moved[:, :LANES]
        return carry

    lax.fori_loop(0, ext_ref.shape[0], one_row, 0)


def conv_group(shifted_ref, taps_ref, first_row, chans):
    sums = [jnp.zeros((GROUP, LANES), F32) for _ in range(ROWS)]
    for col in range(7):
        window = [shifted_ref[col, first_row + r, chans, :] for r in range(ROWS + 6)]
        for row in range(7):
            weight = taps_ref[row * 7 + col, chans, :]
            for i in range(ROWS):
                sums[i] = sums[i] + weight * window[i + row]
    return sums


def gelu_parts(v):
    bell = jnp.exp(v * v * -0.5)
    t = 1.0 / (1.0 + (0.3275911 / math.sqrt(2.0)) * jnp.abs(v))
    poly = t * (
        0.127414796
        + t * (-0.142248368 + t * (0.7107068705 + t * (-0.7265760135 + t * 0.5307027145)))
    )
    tail = poly * bell
    return jnp.where(v < 0.0, tail, 1.0 - tail), bell


def main_kernel(
    ext_ref,
    field_ref,
    cot_ref,
    mask_ref,
    kernel_ref,
    in_ref,
    in_t_ref,
    bias_ref,
    out_ref,
    out_t_ref,
    scale_ref,
    output_ref,
    grad_ref,
    kgrad_ref,
    acc_in_ref,
    acc_out_ref,
    taps_ref,
    shifted_ref,
    kacc_ref,
    conv_ref,
    cgrad_ref,
):
    step = pl.program_id(0)
    channels = conv_ref.shape[0]
    hidden_units = in_ref.shape[1]
    cells = ROWS * LANES
    chunk = 256
    first_row = step * ROWS

    @pl.when(step == 0)
    def _():
        spread_taps(kernel_ref, taps_ref, False)
        shift_rows(ext_ref, shifted_ref)
        kacc_ref[...] = jnp.zeros(kacc_ref.shape, F32)
        acc_in_ref[...] = jnp.zeros(acc_in_ref.shape, F32)
        acc_out_ref[...] = jnp.zeros(acc_out_ref.shape, F32)

    mask = mask_ref[0]
    any_ocean = jnp.max(mask) > 0.0

    @pl.when(jnp.logical_not(any_ocean))
    def _():
        output_ref[...] = jnp.zeros(output_ref.shape, BF16)
        grad_ref[...] = jnp.zeros(grad_ref.shape, BF16)

    @pl.when(any_ocean)
    def _():
        def conv_step(group, carry):
            chans = pl.ds(pl.multiple_of(group * GROUP, GROUP), GROUP)
            sums = conv_group(shifted_ref, taps_ref, first_row, chans)
            for i in range(ROWS):
                conv_ref[chans, i * LANES : (i + 1) * LANES] = sums[i]
            return carry

        lax.fori_loop(0, channels // GROUP, conv_step, 0)

        conv = conv_ref[...]
        centered = conv - jnp.mean(conv, axis=0, keepdims=True)
        variance = jnp.mean(centered * centered, axis=0, keepdims=True)
        inverse = lax.rsqrt(variance + 1e-06)
        normed = centered * inverse
        conv_ref[...] = normed
        normed_half = normed.astype(BF16)
        scale = scale_ref[...]
        cot = jnp.concatenate([cot_ref[i] for i in range(ROWS)], axis=1).astype(F32)
        branch_grad = (scale * (mask * cot)).astype(BF16)
        branch = jnp.zeros((channels, cells), F32)
        normed_grad = jnp.zeros((channels, cells), F32)
        last_dims = (((1,), (1,)), ((), ()))
        for start in range(0, hidden_units, chunk):
            part = slice(start, start + chunk)
            pre_act = (
                jnp.dot(in_t_ref[part, :], normed_half, preferred_element_type=F32)
                + bias_ref[part, :]
            )
            phi, bell = gelu_parts(pre_act)
            hidden = (pre_act * phi).astype(BF16)
            hidden_grad = jnp.dot(out_ref[part, :], branch_grad, preferred_element_type=F32)
            slope = phi + pre_act * bell * (1.0 / math.sqrt(2.0 * math.pi))
            pre_grad = (hidden_grad * slope).astype(BF16)
            branch = branch + jnp.dot(out_t_ref[:, part], hidden, preferred_element_type=F32)
            normed_grad = normed_grad + jnp.dot(
                in_ref[:, part], pre_grad, preferred_element_type=F32
            )
            acc_out_ref[part, :] += lax.dot_general(
                hidden, branch_grad, last_dims, preferred_element_type=F32
            )
            acc_in_ref[:, part] += lax.dot_general(
                normed_half, pre_grad, last_dims, preferred_element_type=F32
            )
        field = jnp.concatenate([field_ref[i] for i in range(ROWS)], axis=1).astype(F32)
        output = (mask * (field + scale * branch)).astype(BF16)
        normed = conv_ref[...]
        mean_grad = jnp.mean(normed_grad, axis=0, keepdims=True)
        mean_prod = jnp.mean(normed_grad * normed, axis=0, keepdims=True)
        conv_grad = (inverse * (normed_grad - mean_grad - normed * mean_prod)).astype(BF16)
        for i in range(ROWS):
            lanes = slice(i * LANES, (i + 1) * LANES)
            output_ref[i] = output[:, lanes]
            grad_ref[i] = conv_grad[:, lanes]
            cgrad_ref[i] = conv_grad[:, lanes].astype(F32)

        def kernel_step(group, carry):
            chans = pl.ds(pl.multiple_of(group * GROUP, GROUP), GROUP)
            grads = [cgrad_ref[i, chans, :] for i in range(ROWS)]
            for col in range(7):
                window = [shifted_ref[col, first_row + r, chans, :] for r in range(ROWS + 6)]
                for row in range(7):
                    total = grads[0] * window[row]
                    for i in range(1, ROWS):
                        total = total + grads[i] * window[i + row]
                    kacc_ref[row * 7 + col, chans, :] += total
            return carry

        lax.fori_loop(0, channels // GROUP, kernel_step, 0)

    @pl.when(step == pl.num_programs(0) - 1)
    def _():
        def reduce_step(group, carry):
            chans = pl.ds(pl.multiple_of(group * GROUP, GROUP), GROUP)
            lane = lax.broadcasted_iota(jnp.int32, (GROUP, LANES), 1)
            table = jnp.zeros((GROUP, LANES), F32)
            for tap in range(49):
                total = jnp.sum(kacc_ref[tap, chans, :], axis=1, keepdims=True)
                table = jnp.where(lane == tap, total, table)
            kgrad_ref[chans, :] = table
            return carry

        lax.fori_loop(0, channels // GROUP, reduce_step, 0)


def field_kernel(ext_ref, cot_ref, mask_ref, kernel_ref, result_ref, taps_ref, shifted_ref):
    step = pl.program_id(0)
    channels = taps_ref.shape[1]
    first_row = step * ROWS

    @pl.when(step == 0)
    def _():
        spread_taps(kernel_ref, taps_ref, True)
        shift_rows(ext_ref, shifted_ref)

    def conv_step(group, carry):
        chans = pl.ds(pl.multiple_of(group * GROUP, GROUP), GROUP)
        sums = conv_group(shifted_ref, taps_ref, first_row, chans)
        for i in range(ROWS):
            mask = mask_ref[0, :, i * LANES : (i + 1) * LANES]
            grad = mask * cot_ref[i, chans, :].astype(F32)
            result_ref[i, chans, :] = (grad + sums[i]).astype(BF16)
        return carry

    lax.fori_loop(0, channels // GROUP, conv_step, 0)


def whole(shape):
    return pl.BlockSpec(shape, lambda step: (0,) * len(shape))


def per_device(
    state_field,
    cotangent,
    ocean_mask,
    kernel,
    inward_weight,
    inward_bias,
    outward_weight,
    layer_scale,
):
    channels, height, width = state_field.shape
    hidden_units = inward_weight.shape[1]
    steps = height // ROWS
    factor = 1.0 / math.sqrt(height * width)
    field = jnp.transpose(state_field, (1, 0, 2))
    cot = jnp.transpose(cotangent, (1, 0, 2))
    mask = ocean_mask.astype(F32).reshape(steps, 1, ROWS * width)
    table = jnp.pad(kernel.reshape(channels, 49), ((0, 0), (0, LANES - 49)))
    ext_shape = (height + 6, channels, WIDE)
    block = pl.BlockSpec((ROWS, channels, width), lambda step: (step, 0, 0))
    mask_block = pl.BlockSpec((1, 1, ROWS * width), lambda step: (step, 0, 0))
    plane = jax.ShapeDtypeStruct((height, channels, width), BF16)
    big = [
        pltpu.VMEM((49, channels, width), F32),
        pltpu.VMEM((7, height + 6, channels, width), F32),
    ]
    params = pltpu.CompilerParams(
        dimension_semantics=("arbitrary",), vmem_limit_bytes=54 * 1024 * 1024
    )
    output, conv_grad, kernel_part, acc_in, acc_out = pl.pallas_call(
        main_kernel,
        grid=(steps,),
        in_specs=[
            whole(ext_shape),
            block,
            block,
            mask_block,
            whole((channels, LANES)),
            whole((channels, hidden_units)),
            whole((hidden_units, channels)),
            whole((hidden_units, 1)),
            whole((hidden_units, channels)),
            whole((channels, hidden_units)),
            whole((channels, 1)),
        ],
        out_specs=[
            block,
            block,
            whole((channels, LANES)),
            whole((channels, hidden_units)),
            whole((hidden_units, channels)),
        ],
        out_shape=[
            plane,
            plane,
            jax.ShapeDtypeStruct((channels, LANES), F32),
            jax.ShapeDtypeStruct((channels, hidden_units), F32),
            jax.ShapeDtypeStruct((hidden_units, channels), F32),
        ],
        scratch_shapes=big
        + [
            pltpu.VMEM((49, channels, width), F32),
            pltpu.VMEM((channels, ROWS * width), F32),
            pltpu.VMEM((ROWS, channels, width), F32),
        ],
        compiler_params=params,
    )(
        extend(field),
        field,
        cot,
        mask,
        table,
        inward_weight,
        inward_weight.T,
        inward_bias[:, None],
        outward_weight,
        outward_weight.T,
        layer_scale[:, None],
    )
    summed = lax.psum((acc_in, acc_out, kernel_part), ("gx", "gy"))
    field_grad = pl.pallas_call(
        field_kernel,
        grid=(steps,),
        in_specs=[whole(ext_shape), block, mask_block, whole((channels, LANES))],
        out_specs=block,
        out_shape=plane,
        scratch_shapes=big,
        compiler_params=params,
        cost_estimate=pl.CostEstimate(
            flops=98 * channels * height * width, bytes_accessed=6000000, transcendentals=0
        ),
    )(extend(conv_grad), cot, mask, table)
    kernel_grad = (summed[2][:, :49] * factor).reshape(channels, 7, 7)
    return (
        jnp.transpose(output, (1, 0, 2)),
        jnp.transpose(field_grad, (1, 0, 2)),
        kernel_grad,
        summed[0] * factor,
        summed[1] * factor,
    )


def solution(mesh):
    in_specs = (P(None, "gy", "gx"), P(None, "gy", "gx"), P("gy", "gx"), P(), P(), P(), P(), P())
    out_specs = (P(None, "gy", "gx"), P(None, "gy", "gx"), P(), P(), P())
    return jax.shard_map(
        per_device, mesh=mesh, in_specs=in_specs, out_specs=out_specs, check_vma=False
    )
```

```python
import functools
import math

import jax
import jax.numpy as jnp
from jax import lax
from jax.experimental import pallas as pl
from jax.experimental.pallas import tpu as pltpu
from jax.sharding import PartitionSpec as P

ROWS = 4
GROUP = 16
LANES = 128
WIDE = 256
F32 = jnp.float32
BF16 = jnp.bfloat16


def extend(rows):
    height, channels, width = rows.shape
    nx = lax.axis_size("gx")
    ny = lax.axis_size("gy")
    top = rows[height - 3 :]
    bottom = rows[:3]
    south = lax.ppermute(top, "gy", [(i, i + 1) for i in range(ny - 1)])
    north = lax.ppermute(bottom, "gy", [(i + 1, i) for i in range(ny - 1)])
    last = ny - 1
    facing = lax.ppermute(
        top, ("gx", "gy"), [(i * ny + last, (nx - 1 - i) * ny + last) for i in range(nx)]
    )
    turn = jnp.flip(jnp.eye(width, dtype=BF16), 0)
    turned = jnp.dot(facing[::-1].reshape(3 * channels, width), turn, preferred_element_type=F32)
    north = north + turned.astype(BF16).reshape(3, channels, width)
    tall = jnp.concatenate([south, rows, north], axis=0)

    def pack(part):
        return jnp.transpose(part, (0, 2, 1)).reshape((height + 6) * 3, channels)

    def unpack(part):
        return jnp.transpose(part.reshape(height + 6, 3, channels), (0, 2, 1))

    left = lax.ppermute(
        pack(tall[:, :, width - 3 :]), "gx", [(i, (i + 1) % nx) for i in range(nx)]
    )
    right = lax.ppermute(pack(tall[:, :, :3]), "gx", [((i + 1) % nx, i) for i in range(nx)])
    spare = jnp.zeros((height + 6, channels, WIDE - width - 6), BF16)
    return jnp.concatenate([unpack(left), tall, unpack(right), spare], axis=2)


def spread_taps(kernel_ref, taps_ref, flipped):
    table = kernel_ref[...]
    for tap in range(49):
        source = 48 - tap if flipped else tap
        taps_ref[tap] = jnp.broadcast_to(table[:, source : source + 1], taps_ref.shape[1:])


def shift_rows(ext_ref, shifted_ref):
    def one_row(row, carry):
        wide = ext_ref[row].astype(F32)
        for tap in range(7):
            moved = wide if tap == 0 else pltpu.roll(wide, WIDE - tap, 1)
            shifted_ref[tap, row] = moved[:, :LANES]
        return carry

    lax.fori_loop(0, ext_ref.shape[0], one_row, 0)


def conv_group(shifted_ref, taps_ref, first_row, chans):
    sums = [jnp.zeros((GROUP, LANES), F32) for _ in range(ROWS)]
    for col in range(7):
        window = [shifted_ref[col, first_row + r, chans, :] for r in range(ROWS + 6)]
        for row in range(7):
            weight = taps_ref[row * 7 + col, chans, :]
            for i in range(ROWS):
                sums[i] = sums[i] + weight * window[i + row]
    return sums


def gelu_parts(v):
    bell = jnp.exp(v * v * -0.5)
    t = 1.0 / (1.0 + (0.3275911 / math.sqrt(2.0)) * jnp.abs(v))
    poly = t * (
        0.127414796
        + t * (-0.142248368 + t * (0.7107068705 + t * (-0.7265760135 + t * 0.5307027145)))
    )
    tail = poly * bell
    return jnp.where(v < 0.0, tail, 1.0 - tail), bell


def main_kernel(
    ext_ref,
    field_ref,
    cot_ref,
    mask_ref,
    kernel_ref,
    in_ref,
    in_t_ref,
    bias_ref,
    out_ref,
    out_t_ref,
    scale_ref,
    output_ref,
    grad_ref,
    acc_ref,
    taps_ref,
    shifted_ref,
    kacc_ref,
    conv_ref,
    cgrad_ref,
):
    step = pl.program_id(0)
    channels = conv_ref.shape[0]
    hidden_units = in_ref.shape[1]
    cells = ROWS * LANES
    chunk = 256
    first_row = step * ROWS

    @pl.when(step == 0)
    def _():
        spread_taps(kernel_ref, taps_ref, False)
        shift_rows(ext_ref, shifted_ref)
        kacc_ref[...] = jnp.zeros(kacc_ref.shape, F32)
        acc_ref[...] = jnp.zeros(acc_ref.shape, F32)

    mask = mask_ref[0]
    any_ocean = jnp.max(mask) > 0.0

    @pl.when(jnp.logical_not(any_ocean))
    def _():
        output_ref[...] = jnp.zeros(output_ref.shape, BF16)
        grad_ref[...] = jnp.zeros(grad_ref.shape, BF16)

    @pl.when(any_ocean)
    def _():
        def conv_step(group, carry):
            chans = pl.ds(pl.multiple_of(group * GROUP, GROUP), GROUP)
            sums = conv_group(shifted_ref, taps_ref, first_row, chans)
            for i in range(ROWS):
                conv_ref[chans, i * LANES : (i + 1) * LANES] = sums[i]
            return carry

        lax.fori_loop(0, channels // GROUP, conv_step, 0)

        conv = conv_ref[...]
        centered = conv - jnp.mean(conv, axis=0, keepdims=True)
        variance = jnp.mean(centered * centered, axis=0, keepdims=True)
        inverse = lax.rsqrt(variance + 1e-06)
        normed = centered * inverse
        conv_ref[...] = normed
        normed_half = normed.astype(BF16)
        scale = scale_ref[...]
        cot = jnp.concatenate([cot_ref[i] for i in range(ROWS)], axis=1).astype(F32)
        branch_grad = (scale * (mask * cot)).astype(BF16)
        branch = jnp.zeros((channels, cells), F32)
        normed_grad = jnp.zeros((channels, cells), F32)
        last_dims = (((1,), (1,)), ((), ()))
        for start in range(0, hidden_units, chunk):
            part = slice(start, start + chunk)
            pre_act = (
                jnp.dot(in_t_ref[part, :], normed_half, preferred_element_type=F32)
                + bias_ref[part, :]
            )
            phi, bell = gelu_parts(pre_act)
            hidden = (pre_act * phi).astype(BF16)
            hidden_grad = jnp.dot(out_ref[part, :], branch_grad, preferred_element_type=F32)
            slope = phi + pre_act * bell * (1.0 / math.sqrt(2.0 * math.pi))
            pre_grad = (hidden_grad * slope).astype(BF16)
            branch = branch + jnp.dot(out_t_ref[:, part], hidden, preferred_element_type=F32)
            normed_grad = normed_grad + jnp.dot(
                in_ref[:, part], pre_grad, preferred_element_type=F32
            )
            in_part = lax.dot_general(
                normed_half, pre_grad, last_dims, preferred_element_type=F32
            )
            out_part = lax.dot_general(
                branch_grad, hidden, last_dims, preferred_element_type=F32
            )
            for first, value in ((0, in_part), (hidden_units // LANES, out_part)):
                for k in range(chunk // LANES):
                    at = (first + start // LANES + k) * channels
                    acc_ref[at : at + channels, :] += value[:, k * LANES : (k + 1) * LANES]
        field = jnp.concatenate([field_ref[i] for i in range(ROWS)], axis=1).astype(F32)
        output = (mask * (field + scale * branch)).astype(BF16)
        normed = conv_ref[...]
        mean_grad = jnp.mean(normed_grad, axis=0, keepdims=True)
        mean_prod = jnp.mean(normed_grad * normed, axis=0, keepdims=True)
        conv_grad = (inverse * (normed_grad - mean_grad - normed * mean_prod)).astype(BF16)
        for i in range(ROWS):
            lanes = slice(i * LANES, (i + 1) * LANES)
            output_ref[i] = output[:, lanes]
            grad_ref[i] = conv_grad[:, lanes]
            cgrad_ref[i] = conv_grad[:, lanes].astype(F32)

        def kernel_step(group, carry):
            chans = pl.ds(pl.multiple_of(group * GROUP, GROUP), GROUP)
            grads = [cgrad_ref[i, chans, :] for i in range(ROWS)]
            for col in range(7):
                window = [shifted_ref[col, first_row + r, chans, :] for r in range(ROWS + 6)]
                for row in range(7):
                    total = grads[0] * window[row]
                    for i in range(1, ROWS):
                        total = total + grads[i] * window[i + row]
                    kacc_ref[row * 7 + col, chans, :] += total
            return carry

        lax.fori_loop(0, channels // GROUP, kernel_step, 0)

    @pl.when(step == pl.num_programs(0) - 1)
    def _():
        def reduce_step(group, carry):
            chans = pl.ds(pl.multiple_of(group * GROUP, GROUP), GROUP)
            lane = lax.broadcasted_iota(jnp.int32, (GROUP, LANES), 1)
            table = jnp.zeros((GROUP, LANES), F32)
            for tap in range(49):
                total = jnp.sum(kacc_ref[tap, chans, :], axis=1, keepdims=True)
                table = jnp.where(lane == tap, total, table)
            at = 2 * (hidden_units // LANES) * channels + group * GROUP
            acc_ref[pl.ds(pl.multiple_of(at, GROUP), GROUP), :] = table
            return carry

        lax.fori_loop(0, channels // GROUP, reduce_step, 0)


def field_kernel(ext_ref, cot_ref, mask_ref, kernel_ref, result_ref, taps_ref, shifted_ref):
    step = pl.program_id(0)
    channels = taps_ref.shape[1]
    first_row = step * ROWS

    @pl.when(step == 0)
    def _():
        spread_taps(kernel_ref, taps_ref, True)
        shift_rows(ext_ref, shifted_ref)

    def conv_step(group, carry):
        chans = pl.ds(pl.multiple_of(group * GROUP, GROUP), GROUP)
        sums = conv_group(shifted_ref, taps_ref, first_row, chans)
        for i in range(ROWS):
            mask = mask_ref[0, :, i * LANES : (i + 1) * LANES]
            grad = mask * cot_ref[i, chans, :].astype(F32)
            result_ref[i, chans, :] = (grad + sums[i]).astype(BF16)
        return carry

    lax.fori_loop(0, channels // GROUP, conv_step, 0)


def sum_kernel(route, factor, part_ref, result_ref, held_ref, final_ref, *rest):
    count = len(route)
    inbox = rest[:count]
    send_sem, recv_sem, back_send_sem, back_recv_sem = rest[count:]
    partners = []
    for axis, bit in route:
        me = lax.axis_index(axis)
        mine = (me // (1 << bit)) % 2
        partners.append((mine, {axis: me + (1 - 2 * mine) * (1 << bit)}))
    barrier = pltpu.get_barrier_semaphore()
    for _, target in partners:
        pl.semaphore_signal(
            barrier, inc=1, device_id=target, device_id_type=pl.DeviceIdType.MESH
        )
    pl.semaphore_wait(barrier, count)

    base = 0
    size = part_ref.shape[0]
    source = part_ref
    for k, (mine, target) in enumerate(partners):
        size = size // 2
        keep = pl.ds(pl.multiple_of(base + mine * size, 16), size)
        give = pl.ds(pl.multiple_of(base + (1 - mine) * size, 16), size)
        copy = pltpu.make_async_remote_copy(
            src_ref=source.at[give],
            dst_ref=inbox[k],
            send_sem=send_sem.at[k],
            recv_sem=recv_sem.at[k],
            device_id=target,
            device_id_type=pl.DeviceIdType.MESH,
        )
        copy.start()
        copy.wait()
        held_ref[keep, :] = source[keep, :] + inbox[k][...]
        source = held_ref
        base = base + mine * size
    own = pl.ds(pl.multiple_of(base, 16), size)
    final_ref[own, :] = (held_ref[own, :] * factor).astype(BF16)
    for k in reversed(range(count)):
        mine, target = partners[k]
        block = pl.ds(pl.multiple_of(base, 16), size)
        copy = pltpu.make_async_remote_copy(
            src_ref=final_ref.at[block],
            dst_ref=final_ref.at[block],
            send_sem=back_send_sem.at[k],
            recv_sem=back_recv_sem.at[k],
            device_id=target,
            device_id_type=pl.DeviceIdType.MESH,
        )
        copy.start()
        copy.wait()
        base = base - mine * size
        size = size * 2
    result_ref[...] = final_ref[...].astype(F32)


def sum_devices(part, factor):
    route = []
    for axis in ("gx", "gy"):
        bits = lax.axis_size(axis).bit_length() - 1
        route += [(axis, bit) for bit in range(bits)]
    rows = part.shape[0]
    count = len(route)
    return pl.pallas_call(
        functools.partial(sum_kernel, tuple(route), factor),
        in_specs=[pl.BlockSpec(memory_space=pltpu.VMEM)],
        out_specs=pl.BlockSpec(memory_space=pltpu.VMEM),
        out_shape=jax.ShapeDtypeStruct(part.shape, F32),
        scratch_shapes=[pltpu.VMEM(part.shape, F32), pltpu.VMEM(part.shape, BF16)]
        + [pltpu.VMEM((rows >> (k + 1), LANES), F32) for k in range(count)]
        + [pltpu.SemaphoreType.DMA((count,))] * 4,
        compiler_params=pltpu.CompilerParams(
            collective_id=0, has_side_effects=True, vmem_limit_bytes=24 * 1024 * 1024
        ),
    )(part)


def whole(shape):
    return pl.BlockSpec(shape, lambda step: (0,) * len(shape))


def per_device(
    state_field,
    cotangent,
    ocean_mask,
    kernel,
    inward_weight,
    inward_bias,
    outward_weight,
    layer_scale,
):
    channels, height, width = state_field.shape
    hidden_units = inward_weight.shape[1]
    steps = height // ROWS
    factor = 1.0 / math.sqrt(height * width)
    field = jnp.transpose(state_field, (1, 0, 2))
    cot = jnp.transpose(cotangent, (1, 0, 2))
    mask = ocean_mask.astype(F32).reshape(steps, 1, ROWS * width)
    table = jnp.pad(kernel.reshape(channels, 49), ((0, 0), (0, LANES - 49)))
    ext_shape = (height + 6, channels, WIDE)
    block = pl.BlockSpec((ROWS, channels, width), lambda step: (step, 0, 0))
    mask_block = pl.BlockSpec((1, 1, ROWS * width), lambda step: (step, 0, 0))
    plane = jax.ShapeDtypeStruct((height, channels, width), BF16)
    big = [
        pltpu.VMEM((49, channels, width), F32),
        pltpu.VMEM((7, height + 6, channels, width), F32),
    ]
    params = pltpu.CompilerParams(
        dimension_semantics=("arbitrary",), vmem_limit_bytes=54 * 1024 * 1024
    )
    blocks = hidden_units // LANES
    used = (2 * blocks + 1) * channels
    share = GROUP * lax.axis_size("gx") * lax.axis_size("gy")
    total = -(-used // share) * share
    output, conv_grad, acc = pl.pallas_call(
        main_kernel,
        grid=(steps,),
        in_specs=[
            whole(ext_shape),
            block,
            block,
            mask_block,
            whole((channels, LANES)),
            whole((channels, hidden_units)),
            whole((hidden_units, channels)),
            whole((hidden_units, 1)),
            whole((hidden_units, channels)),
            whole((channels, hidden_units)),
            whole((channels, 1)),
        ],
        out_specs=[
            block,
            block,
            whole((total, LANES)),
        ],
        out_shape=[
            plane,
            plane,
            jax.ShapeDtypeStruct((total, LANES), F32),
        ],
        scratch_shapes=big
        + [
            pltpu.VMEM((49, channels, width), F32),
            pltpu.VMEM((channels, ROWS * width), F32),
            pltpu.VMEM((ROWS, channels, width), F32),
        ],
        compiler_params=params,
    )(
        extend(field),
        field,
        cot,
        mask,
        table,
        inward_weight,
        inward_weight.T,
        inward_bias[:, None],
        outward_weight,
        outward_weight.T,
        layer_scale[:, None],
    )
    summed = sum_devices(acc, factor)[:used].reshape(2 * blocks + 1, channels, LANES)
    inward_grad = jnp.transpose(summed[:blocks], (1, 0, 2)).reshape(channels, hidden_units)
    outward_grad = jnp.transpose(summed[blocks : 2 * blocks], (0, 2, 1)).reshape(
        hidden_units, channels
    )
    field_grad = pl.pallas_call(
        field_kernel,
        grid=(steps,),
        in_specs=[whole(ext_shape), block, mask_block, whole((channels, LANES))],
        out_specs=block,
        out_shape=plane,
        scratch_shapes=big,
        compiler_params=params,
        cost_estimate=pl.CostEstimate(
            flops=98 * channels * height * width, bytes_accessed=6000000, transcendentals=0
        ),
    )(extend(conv_grad), cot, mask, table)
    kernel_grad = summed[2 * blocks, :, :49].reshape(channels, 7, 7)
    return (
        jnp.transpose(output, (1, 0, 2)),
        jnp.transpose(field_grad, (1, 0, 2)),
        kernel_grad,
        inward_grad,
        outward_grad,
    )


def solution(mesh):
    in_specs = (P(None, "gy", "gx"), P(None, "gy", "gx"), P("gy", "gx"), P(), P(), P(), P(), P())
    out_specs = (P(None, "gy", "gx"), P(None, "gy", "gx"), P(), P(), P())
    return jax.shard_map(
        per_device, mesh=mesh, in_specs=in_specs, out_specs=out_specs, check_vma=False
    )
```

```python
import functools
import math

import jax
import jax.numpy as jnp
from jax import lax
from jax.experimental import pallas as pl
from jax.experimental.pallas import tpu as pltpu
from jax.sharding import PartitionSpec as P

ROWS = 4
GROUP = 16
LANES = 128
WIDE = 256
F32 = jnp.float32
BF16 = jnp.bfloat16


def extend(rows):
    height, channels, width = rows.shape
    nx = lax.axis_size("gx")
    ny = lax.axis_size("gy")
    top = rows[height - 3 :]
    bottom = rows[:3]
    south = lax.ppermute(top, "gy", [(i, i + 1) for i in range(ny - 1)])
    north = lax.ppermute(bottom, "gy", [(i + 1, i) for i in range(ny - 1)])
    last = ny - 1
    facing = lax.ppermute(
        top, ("gx", "gy"), [(i * ny + last, (nx - 1 - i) * ny + last) for i in range(nx)]
    )
    turn = jnp.flip(jnp.eye(width, dtype=BF16), 0)
    turned = jnp.dot(facing[::-1].reshape(3 * channels, width), turn, preferred_element_type=F32)
    north = north + turned.astype(BF16).reshape(3, channels, width)
    tall = jnp.concatenate([south, rows, north], axis=0)

    def pack(part):
        return jnp.transpose(part, (0, 2, 1)).reshape((height + 6) * 3, channels)

    def unpack(part):
        return jnp.transpose(part.reshape(height + 6, 3, channels), (0, 2, 1))

    left = lax.ppermute(
        pack(tall[:, :, width - 3 :]), "gx", [(i, (i + 1) % nx) for i in range(nx)]
    )
    right = lax.ppermute(pack(tall[:, :, :3]), "gx", [((i + 1) % nx, i) for i in range(nx)])
    spare = jnp.zeros((height + 6, channels, WIDE - width - 6), BF16)
    return jnp.concatenate([unpack(left), tall, unpack(right), spare], axis=2)


def spread_taps(kernel_ref, taps_ref, flipped):
    table = kernel_ref[...]
    for tap in range(49):
        source = 48 - tap if flipped else tap
        taps_ref[tap] = jnp.broadcast_to(table[:, source : source + 1], taps_ref.shape[1:])


def shift_rows(ext_ref, shifted_ref):
    def one_row(row, carry):
        wide = ext_ref[row].astype(F32)
        for tap in range(7):
            moved = wide if tap == 0 else pltpu.roll(wide, WIDE - tap, 1)
            shifted_ref[tap, row] = moved[:, :LANES]
        return carry

    lax.fori_loop(0, ext_ref.shape[0], one_row, 0)


def conv_group(shifted_ref, taps_ref, first_row, chans):
    sums = [jnp.zeros((GROUP, LANES), F32) for _ in range(ROWS)]
    for col in range(7):
        window = [shifted_ref[col, first_row + r, chans, :] for r in range(ROWS + 6)]
        for row in range(7):
            weight = taps_ref[row * 7 + col, chans, :]
            for i in range(ROWS):
                sums[i] = sums[i] + weight * window[i + row]
    return sums


def gelu_parts(v):
    bell = jnp.exp(v * v * -0.5)
    t = 1.0 / (1.0 + (0.3275911 / math.sqrt(2.0)) * jnp.abs(v))
    poly = t * (
        0.127414796
        + t * (-0.142248368 + t * (0.7107068705 + t * (-0.7265760135 + t * 0.5307027145)))
    )
    tail = poly * bell
    return jnp.where(v < 0.0, tail, 1.0 - tail), bell


def main_kernel(
    ext_ref,
    field_ref,
    cot_ref,
    mask_ref,
    kernel_ref,
    in_ref,
    in_t_ref,
    bias_ref,
    out_ref,
    out_t_ref,
    scale_ref,
    output_ref,
    grad_ref,
    acc_ref,
    taps_ref,
    shifted_ref,
    kacc_ref,
    conv_ref,
    cgrad_ref,
):
    step = pl.program_id(0)
    channels = conv_ref.shape[0]
    hidden_units = in_ref.shape[1]
    cells = ROWS * LANES
    chunk = 256
    first_row = step * ROWS

    @pl.when(step == 0)
    def _():
        spread_taps(kernel_ref, taps_ref, False)
        shift_rows(ext_ref, shifted_ref)
        kacc_ref[...] = jnp.zeros(kacc_ref.shape, F32)
        acc_ref[...] = jnp.zeros(acc_ref.shape, F32)

    mask = mask_ref[0]
    any_ocean = jnp.max(mask) > 0.0

    @pl.when(jnp.logical_not(any_ocean))
    def _():
        output_ref[...] = jnp.zeros(output_ref.shape, BF16)
        grad_ref[...] = jnp.zeros(grad_ref.shape, BF16)

    @pl.when(any_ocean)
    def _():
        def conv_step(group, carry):
            chans = pl.ds(pl.multiple_of(group * GROUP, GROUP), GROUP)
            sums = conv_group(shifted_ref, taps_ref, first_row, chans)
            for i in range(ROWS):
                conv_ref[chans, i * LANES : (i + 1) * LANES] = sums[i]
            return carry

        lax.fori_loop(0, channels // GROUP, conv_step, 0)

        conv = conv_ref[...]
        centered = conv - jnp.mean(conv, axis=0, keepdims=True)
        variance = jnp.mean(centered * centered, axis=0, keepdims=True)
        inverse = lax.rsqrt(variance + 1e-06)
        normed = centered * inverse
        conv_ref[...] = normed
        normed_half = normed.astype(BF16)
        scale = scale_ref[...]
        cot = jnp.concatenate([cot_ref[i] for i in range(ROWS)], axis=1).astype(F32)
        branch_grad = (scale * (mask * cot)).astype(BF16)
        branch = jnp.zeros((channels, cells), F32)
        normed_grad = jnp.zeros((channels, cells), F32)
        last_dims = (((1,), (1,)), ((), ()))
        for start in range(0, hidden_units, chunk):
            part = slice(start, start + chunk)
            pre_act = (
                jnp.dot(in_t_ref[part, :], normed_half, preferred_element_type=F32)
                + bias_ref[part, :]
            )
            phi, bell = gelu_parts(pre_act)
            hidden = (pre_act * phi).astype(BF16)
            hidden_grad = jnp.dot(out_ref[part, :], branch_grad, preferred_element_type=F32)
            slope = phi + pre_act * bell * (1.0 / math.sqrt(2.0 * math.pi))
            pre_grad = (hidden_grad * slope).astype(BF16)
            branch = branch + jnp.dot(out_t_ref[:, part], hidden, preferred_element_type=F32)
            normed_grad = normed_grad + jnp.dot(
                in_ref[:, part], pre_grad, preferred_element_type=F32
            )
            in_part = lax.dot_general(
                normed_half, pre_grad, last_dims, preferred_element_type=F32
            )
            out_part = lax.dot_general(
                branch_grad, hidden, last_dims, preferred_element_type=F32
            )
            for first, value in ((0, in_part), (hidden_units // LANES, out_part)):
                for k in range(chunk // LANES):
                    at = (first + start // LANES + k) * channels
                    acc_ref[at : at + channels, :] += value[:, k * LANES : (k + 1) * LANES]
        field = jnp.concatenate([field_ref[i] for i in range(ROWS)], axis=1).astype(F32)
        output = (mask * (field + scale * branch)).astype(BF16)
        normed = conv_ref[...]
        mean_grad = jnp.mean(normed_grad, axis=0, keepdims=True)
        mean_prod = jnp.mean(normed_grad * normed, axis=0, keepdims=True)
        conv_grad = (inverse * (normed_grad - mean_grad - normed * mean_prod)).astype(BF16)
        for i in range(ROWS):
            lanes = slice(i * LANES, (i + 1) * LANES)
            output_ref[i] = output[:, lanes]
            grad_ref[i] = conv_grad[:, lanes]
            cgrad_ref[i] = conv_grad[:, lanes].astype(F32)

        def kernel_step(group, carry):
            chans = pl.ds(pl.multiple_of(group * GROUP, GROUP), GROUP)
            grads = [cgrad_ref[i, chans, :] for i in range(ROWS)]
            for col in range(7):
                window = [shifted_ref[col, first_row + r, chans, :] for r in range(ROWS + 6)]
                for row in range(7):
                    total = grads[0] * window[row]
                    for i in range(1, ROWS):
                        total = total + grads[i] * window[i + row]
                    kacc_ref[row * 7 + col, chans, :] += total
            return carry

        lax.fori_loop(0, channels // GROUP, kernel_step, 0)

    @pl.when(step == pl.num_programs(0) - 1)
    def _():
        def reduce_step(group, carry):
            chans = pl.ds(pl.multiple_of(group * GROUP, GROUP), GROUP)
            lane = lax.broadcasted_iota(jnp.int32, (GROUP, LANES), 1)
            table = jnp.zeros((GROUP, LANES), F32)
            for tap in range(49):
                total = jnp.sum(kacc_ref[tap, chans, :], axis=1, keepdims=True)
                table = jnp.where(lane == tap, total, table)
            at = 2 * (hidden_units // LANES) * channels + group * GROUP
            acc_ref[pl.ds(pl.multiple_of(at, GROUP), GROUP), :] = table
            return carry

        lax.fori_loop(0, channels // GROUP, reduce_step, 0)


def field_kernel(ext_ref, cot_ref, mask_ref, kernel_ref, result_ref, taps_ref, shifted_ref):
    step = pl.program_id(0)
    channels = taps_ref.shape[1]
    first_row = step * ROWS

    @pl.when(step == 0)
    def _():
        spread_taps(kernel_ref, taps_ref, True)
        shift_rows(ext_ref, shifted_ref)

    def conv_step(group, carry):
        chans = pl.ds(pl.multiple_of(group * GROUP, GROUP), GROUP)
        sums = conv_group(shifted_ref, taps_ref, first_row, chans)
        for i in range(ROWS):
            mask = mask_ref[0, :, i * LANES : (i + 1) * LANES]
            grad = mask * cot_ref[i, chans, :].astype(F32)
            result_ref[i, chans, :] = (grad + sums[i]).astype(BF16)
        return carry

    lax.fori_loop(0, channels // GROUP, conv_step, 0)


def sum_kernel(route, factor, part_ref, result_ref, held_ref, final_ref, *rest):
    count = len(route)
    inbox = rest[:count]
    outbox = rest[count : 2 * count]
    send_sem, recv_sem, back_send_sem, back_recv_sem = rest[2 * count :]
    partners = []
    for axis, bit in route:
        me = lax.axis_index(axis)
        mine = (me // (1 << bit)) % 2
        partners.append((mine, {axis: me + (1 - 2 * mine) * (1 << bit)}))
    barrier = pltpu.get_barrier_semaphore()
    for _, target in partners:
        pl.semaphore_signal(
            barrier, inc=1, device_id=target, device_id_type=pl.DeviceIdType.MESH
        )
    pl.semaphore_wait(barrier, count)

    base = 0
    size = part_ref.shape[0]
    source = part_ref
    for k, (mine, target) in enumerate(partners):
        size = size // 2
        keep = pl.ds(pl.multiple_of(base + mine * size, 16), size)
        give = pl.ds(pl.multiple_of(base + (1 - mine) * size, 16), size)
        outbox[k][...] = source[give, :].astype(BF16)
        copy = pltpu.make_async_remote_copy(
            src_ref=outbox[k],
            dst_ref=inbox[k],
            send_sem=send_sem.at[k],
            recv_sem=recv_sem.at[k],
            device_id=target,
            device_id_type=pl.DeviceIdType.MESH,
        )
        copy.start()
        copy.wait()
        held_ref[keep, :] = source[keep, :] + inbox[k][...].astype(F32)
        source = held_ref
        base = base + mine * size
    own = pl.ds(pl.multiple_of(base, 16), size)
    final_ref[own, :] = (held_ref[own, :] * factor).astype(BF16)
    for k in reversed(range(count)):
        mine, target = partners[k]
        block = pl.ds(pl.multiple_of(base, 16), size)
        copy = pltpu.make_async_remote_copy(
            src_ref=final_ref.at[block],
            dst_ref=final_ref.at[block],
            send_sem=back_send_sem.at[k],
            recv_sem=back_recv_sem.at[k],
            device_id=target,
            device_id_type=pl.DeviceIdType.MESH,
        )
        copy.start()
        copy.wait()
        base = base - mine * size
        size = size * 2
    result_ref[...] = final_ref[...].astype(F32)


def sum_devices(part, factor):
    route = []
    for axis in ("gx", "gy"):
        bits = lax.axis_size(axis).bit_length() - 1
        route += [(axis, bit) for bit in range(bits)]
    rows = part.shape[0]
    count = len(route)
    return pl.pallas_call(
        functools.partial(sum_kernel, tuple(route), factor),
        in_specs=[pl.BlockSpec(memory_space=pltpu.VMEM)],
        out_specs=pl.BlockSpec(memory_space=pltpu.VMEM),
        out_shape=jax.ShapeDtypeStruct(part.shape, F32),
        scratch_shapes=[pltpu.VMEM(part.shape, F32), pltpu.VMEM(part.shape, BF16)]
        + 2 * [pltpu.VMEM((rows >> (k + 1), LANES), BF16) for k in range(count)]
        + [pltpu.SemaphoreType.DMA((count,))] * 4,
        compiler_params=pltpu.CompilerParams(
            collective_id=0, has_side_effects=True, vmem_limit_bytes=24 * 1024 * 1024
        ),
    )(part)


def whole(shape):
    return pl.BlockSpec(shape, lambda step: (0,) * len(shape))


def per_device(
    state_field,
    cotangent,
    ocean_mask,
    kernel,
    inward_weight,
    inward_bias,
    outward_weight,
    layer_scale,
):
    channels, height, width = state_field.shape
    hidden_units = inward_weight.shape[1]
    steps = height // ROWS
    factor = 1.0 / math.sqrt(height * width)
    field = jnp.transpose(state_field, (1, 0, 2))
    cot = jnp.transpose(cotangent, (1, 0, 2))
    mask = ocean_mask.astype(F32).reshape(steps, 1, ROWS * width)
    table = jnp.pad(kernel.reshape(channels, 49), ((0, 0), (0, LANES - 49)))
    ext_shape = (height + 6, channels, WIDE)
    block = pl.BlockSpec((ROWS, channels, width), lambda step: (step, 0, 0))
    mask_block = pl.BlockSpec((1, 1, ROWS * width), lambda step: (step, 0, 0))
    plane = jax.ShapeDtypeStruct((height, channels, width), BF16)
    big = [
        pltpu.VMEM((49, channels, width), F32),
        pltpu.VMEM((7, height + 6, channels, width), F32),
    ]
    params = pltpu.CompilerParams(
        dimension_semantics=("arbitrary",), vmem_limit_bytes=54 * 1024 * 1024
    )
    blocks = hidden_units // LANES
    used = (2 * blocks + 1) * channels
    share = GROUP * lax.axis_size("gx") * lax.axis_size("gy")
    total = -(-used // share) * share
    output, conv_grad, acc = pl.pallas_call(
        main_kernel,
        grid=(steps,),
        in_specs=[
            whole(ext_shape),
            block,
            block,
            mask_block,
            whole((channels, LANES)),
            whole((channels, hidden_units)),
            whole((hidden_units, channels)),
            whole((hidden_units, 1)),
            whole((hidden_units, channels)),
            whole((channels, hidden_units)),
            whole((channels, 1)),
        ],
        out_specs=[
            block,
            block,
            whole((total, LANES)),
        ],
        out_shape=[
            plane,
            plane,
            jax.ShapeDtypeStruct((total, LANES), F32),
        ],
        scratch_shapes=big
        + [
            pltpu.VMEM((49, channels, width), F32),
            pltpu.VMEM((channels, ROWS * width), F32),
            pltpu.VMEM((ROWS, channels, width), F32),
        ],
        compiler_params=params,
    )(
        extend(field),
        field,
        cot,
        mask,
        table,
        inward_weight,
        inward_weight.T,
        inward_bias[:, None],
        outward_weight,
        outward_weight.T,
        layer_scale[:, None],
    )
    summed = sum_devices(acc, factor)[:used].reshape(2 * blocks + 1, channels, LANES)
    inward_grad = jnp.transpose(summed[:blocks], (1, 0, 2)).reshape(channels, hidden_units)
    outward_grad = jnp.transpose(summed[blocks : 2 * blocks], (0, 2, 1)).reshape(
        hidden_units, channels
    )
    field_grad = pl.pallas_call(
        field_kernel,
        grid=(steps,),
        in_specs=[whole(ext_shape), block, mask_block, whole((channels, LANES))],
        out_specs=block,
        out_shape=plane,
        scratch_shapes=big,
        compiler_params=params,
        cost_estimate=pl.CostEstimate(
            flops=98 * channels * height * width, bytes_accessed=6000000, transcendentals=0
        ),
    )(extend(conv_grad), cot, mask, table)
    kernel_grad = summed[2 * blocks, :, :49].reshape(channels, 7, 7)
    return (
        jnp.transpose(output, (1, 0, 2)),
        jnp.transpose(field_grad, (1, 0, 2)),
        kernel_grad,
        inward_grad,
        outward_grad,
    )


def solution(mesh):
    in_specs = (P(None, "gy", "gx"), P(None, "gy", "gx"), P("gy", "gx"), P(), P(), P(), P(), P())
    out_specs = (P(None, "gy", "gx"), P(None, "gy", "gx"), P(), P(), P())
    return jax.shard_map(
        per_device, mesh=mesh, in_specs=in_specs, out_specs=out_specs, check_vma=False
    )
```
